32 devices in a mesh: groups: 2 (over y), row: 4 (over z), col: 4 (over x, core).
Axes of the slice: x: 2, y: 2, z: 4, core: 2. Of those that a mesh axis runs over, the one named last changes fastest.
Arguments:
- green_starting_blocks: float32 [4, 128, 2048], P('groups', None, ('row', 'col')), parts along dimension 0, may hold values from -3 to 3
- fit_vectors: bfloat16 [256, 4096], P('groups'), parts along dimension 0, may hold values from -0.75 to 0.75
- history: bfloat16 [4, 2048, 2048], P('groups', 'row', 'col'), parts along dimension 0, may hold values from -0.125 to 0.125
Outputs:
- green_final: float32 [4, 128, 2048], P('groups', None, ('row', 'col')), parts along dimension 0
The draws below stay inside these ranges and needn't reach their ends.
There are 2 independent parts, one for each index of `groups`. The reference program is written for one: setup_inputs(seed, part) draws one part's arguments, and reference() takes and returns one part's arrays. A program takes and returns all parts, laid end to end along the dimension named above; each array names one. Nothing has to cross between parts.
All inputs are finite; a program needn't handle non-finite values.
Results may differ from the reference program's by a relative error of at most 0.03.
Values may be sent and summed in bfloat16 or wider, within the bound.
No kernel may reach another device: no remote copies, remote signals or barrier semaphores. Data moves between devices by JAX's collectives and lax.ppermute only.
A program may use at most 128 MiB of HBM per device.

```python
import jax
import jax.numpy as jnp
from jax import lax

NO = 64
NAUX = 128
NEW = 2
ITERS = 2
PAST = 32
SLICE_ROWS = 128
ORDER = 2048


def strengthened(array, own_key, source, target, blocks, factor):
    owner, partner = [(jnp.arange(array.shape[axis_at]) // (array.shape[axis_at] // blocks)).reshape([-1 if axis == axis_at else 1 for axis in range(array.ndim)]) for axis_at in (source, target)]
    chosen = jax.random.permutation(own_key, blocks)[partner]
    strong = (owner == chosen) | (owner == (partner + blocks // 2) % blocks)
    return jnp.where(strong, factor * array, array)


def steps_of(key, shape, pieces, smallest, high):
    gain = 1.0
    for dim, blocks in pieces:
        steps = jax.random.uniform(jax.random.fold_in(jax.random.fold_in(key, 6), dim), (blocks,), jnp.float32, smallest / len(pieces), high / len(pieces))
        gain = gain * jnp.repeat(jnp.exp(steps), shape[dim] // blocks).reshape((-1,) + (1,) * (len(shape) - 1 - dim))
    return gain


def gaussian(rng, extent, spread, limit, split=(), kind=jnp.bfloat16):
    entries = spread * jax.random.normal(rng, extent, jnp.float32)
    if split:
        entries = entries * steps_of(rng, extent, split, -0.22, 0.18)
    return jnp.clip(entries, -limit, limit).astype(kind)


def bell_draw_with(own_key, extent, deviation, bound, split, heavy, kind=jnp.bfloat16):
    array = deviation * jax.random.normal(own_key, extent, jnp.float32)
    if split:
        array = array * steps_of(own_key, extent, split, -0.22, 0.18)
    return jnp.clip(strengthened(array, jax.random.fold_in(own_key, 3), *heavy), -bound, bound).astype(kind)


def setup_inputs(seed: int = 0, part: int = 0) -> dict:
    seeds = jax.random.split(jax.random.key(seed), 4)
    part_splits = jax.random.split(jax.random.fold_in(seeds[3], part), 4)
    return {
        "green_starting_blocks": gaussian(part_splits[0], (2, SLICE_ROWS, ORDER), 0.5, 3.0, ((2, 16),), jnp.float32),
        "fit_vectors": gaussian(part_splits[1], (NAUX, NO * NO), NO ** -0.5, 0.75),
        "history": bell_draw_with(part_splits[2], (2, ORDER, ORDER), (2 * ORDER) ** -0.5, 0.125, ((1, 4), (2, 4)), (1, 2, 4, 2.0)),
    }


def pair_self_energy(pair_blocks, fit_vectors):
    pair_count = pair_blocks.shape[1]
    orbitals = pair_blocks.shape[2]
    aux_count = fit_vectors.shape[0]
    lowered = pair_blocks.astype(jnp.bfloat16)
    fit_basis = fit_vectors.reshape(aux_count * orbitals, orbitals)
    inner_side = jnp.transpose(lowered, (2, 0, 1, 3)).reshape(orbitals, 2 * pair_count * orbitals)
    left_prod = jnp.dot(fit_basis, inner_side, preferred_element_type=jnp.float32).astype(jnp.bfloat16)
    left_prod = left_prod.reshape(aux_count, orbitals, 2, pair_count, orbitals)
    fit_turned = jnp.transpose(fit_vectors.reshape(aux_count, orbitals, orbitals), (1, 0, 2)).reshape(orbitals, aux_count * orbitals)
    right_prod = jnp.dot(lowered.reshape(2 * pair_count * orbitals, orbitals), fit_turned, preferred_element_type=jnp.float32).astype(jnp.bfloat16)
    right_prod = right_prod.reshape(2, pair_count, orbitals, aux_count, orbitals)
    bubble = jnp.einsum("picnk,cniqk->npq", left_prod.astype(jnp.float32), right_prod.astype(jnp.float32)) / orbitals
    bubble = bubble.astype(jnp.bfloat16)
    screened = jnp.einsum("npq,qm->npm", bubble.astype(jnp.float32), fit_vectors.astype(jnp.float32)).astype(jnp.bfloat16)
    screened = screened.reshape(pair_count, aux_count, orbitals, orbitals)
    scale_factor = (aux_count * orbitals) ** -0.5
    energy = jnp.einsum("picnl,nplj->cnij", left_prod.astype(jnp.float32), screened.astype(jnp.float32)) * scale_factor
    return energy.astype(jnp.bfloat16)


def reference(green_starting_blocks, fit_vectors, history):
    green_current = green_starting_blocks

    def per_time(time_block):
        return pair_self_energy(time_block, fit_vectors)

    for iteration in range(ITERS):
        time_blocks = green_current.reshape(2, NEW, NO, PAST, NO).transpose(3, 0, 1, 2, 4)
        energies = lax.map(per_time, time_blocks)
        self_energy = energies.transpose(1, 2, 3, 0, 4).reshape(2, SLICE_ROWS, ORDER)
        stacked = self_energy.reshape(2 * SLICE_ROWS, ORDER)
        real_half = jnp.dot(stacked, history[0], preferred_element_type=jnp.float32)
        imaginary_half = jnp.dot(stacked, history[1], preferred_element_type=jnp.float32)
        collision_real = real_half[:SLICE_ROWS] - imaginary_half[SLICE_ROWS:]
        collision_imaginary = imaginary_half[:SLICE_ROWS] + real_half[SLICE_ROWS:]
        green_current = green_starting_blocks + jnp.stack([collision_real, collision_imaginary])
    return green_current
```

```python
import functools
import math

import jax
import jax.numpy as jnp
from jax import lax
from jax.experimental import pallas as pl
from jax.experimental.pallas import tpu as pltpu
from jax.sharding import PartitionSpec as P

ITERS = 2
BF16 = jnp.bfloat16
F32 = jnp.float32
LANES = 128
MIB = 2**20


def dot(a, b):
    return jnp.dot(a, b, preferred_element_type=F32)


def dot_nt(a, b):
    return lax.dot_general(a, b, (((1,), (1,)), ((), ())), preferred_element_type=F32)


def turn_kernel(orbitals, fit_ref, turned_ref, wide):
    flat = fit_ref.shape[1]
    per = LANES // orbitals
    for t in range(flat // LANES):
        wide[t * LANES : (t + 1) * LANES, :] = fit_ref[:, t * LANES : (t + 1) * LANES].astype(F32).T
    for t in range(flat // LANES):
        rows = [wide[pl.ds(t * per + h, orbitals, stride=orbitals), :] for h in range(per)]
        turned_ref[:, t * LANES : (t + 1) * LANES] = jnp.concatenate(rows, axis=0).T.astype(BF16)


def turn(fit, orbitals):
    aux, flat = fit.shape
    return pl.pallas_call(
        functools.partial(turn_kernel, orbitals),
        out_shape=jax.ShapeDtypeStruct((aux, flat), BF16),
        scratch_shapes=[pltpu.VMEM((flat, aux), F32)],
        compiler_params=pltpu.CompilerParams(vmem_limit_bytes=16 * MIB),
        name="turn_fit",
    )(fit)


def energy_kernel(orbitals, green_ref, fit_ref, turned_ref, out_ref, spread, left, under, screened):
    aux = fit_ref.shape[0]
    times = green_ref.shape[2] // orbitals
    new = green_ref.shape[1] // orbitals
    pairs = new * times
    pitch = 2 * orbitals + 1
    per = LANES // orbitals
    flipped = [
        [green_ref[c, a * orbitals : (a + 1) * orbitals, :].T.astype(BF16) for c in range(2)]
        for a in range(new)
    ]
    lhs = jnp.concatenate([flipped[a][c] for a in range(new) for c in range(2)], axis=0)
    zero = jnp.zeros_like(lhs)
    both = [
        jnp.concatenate([lhs if q == h else zero for q in range(per)], axis=1) for h in range(per)
    ]
    for i in range(0, orbitals, 2 * per):
        w = jnp.concatenate(
            [fit_ref[:, (i + per * g) * orbitals : (i + per * (g + 1)) * orbitals] for g in range(2)],
            axis=0,
        )
        for h in range(per):
            res = dot_nt(both[h], w)
            for g in range(2):
                for a in range(new):
                    for c in range(2):
                        for k in range(times):
                            r = ((a * 2 + c) * times + k) * orbitals
                            spread[
                                a * times + k,
                                pl.ds(c * orbitals + i + per * g + h, orbitals, stride=pitch),
                                :,
                            ] = res[r : r + orbitals, g * aux : (g + 1) * aux]
    around = [jnp.concatenate(flipped[a], axis=1) for a in range(new)]
    rows = 2 * orbitals
    for m in range(0, orbitals, 2):
        for n in range(pairs):
            a, k = divmod(n, times)
            x = [spread[n, pl.ds((m + h) * pitch, rows), :].astype(BF16) for h in range(2)]
            for h in range(2):
                left[n, (m + h) * rows : (m + h + 1) * rows, :] = x[h]
            r = dot(around[a][k * orbitals : (k + 1) * orbitals], jnp.concatenate(x, axis=1))
            for h in range(2):
                under[(m + h) * orbitals : (m + h + 1) * orbitals, n * aux : (n + 1) * aux] = r[
                    :, h * aux : (h + 1) * aux
                ].astype(BF16)
    pi = dot(turned_ref[...], under[...]) * (1.0 / orbitals)
    bubble = jnp.concatenate([pi[:, n * aux : (n + 1) * aux].T for n in range(pairs)], axis=0)
    screened[...] = dot(bubble.astype(BF16), fit_ref[...]).astype(BF16)
    scale = (aux * orbitals) ** -0.5
    accs = [jnp.zeros((rows, orbitals), F32) for _ in range(pairs)]
    for m in range(0, orbitals, 2):
        for n in range(pairs):
            a = jnp.concatenate(
                [left[n, (m + h) * rows : (m + h + 1) * rows, :] for h in range(2)], axis=1
            )
            w = screened[n * aux : (n + 1) * aux, m * orbitals : (m + 2) * orbitals]
            b = jnp.concatenate([w[:, :orbitals], w[:, orbitals:]], axis=0)
            accs[n] = accs[n] + dot(a, b)
    for n in range(pairs):
        a, k = divmod(n, times)
        block = (accs[n] * scale).astype(BF16)
        for c in range(2):
            out_ref[
                c, a * orbitals : (a + 1) * orbitals, k * orbitals : (k + 1) * orbitals
            ] = block[c * orbitals : (c + 1) * orbitals]


def energy(green, fit, turned, orbitals):
    aux, flat = fit.shape
    _, rows, span = green.shape
    pairs = rows // orbitals * (span // orbitals)
    return pl.pallas_call(
        functools.partial(energy_kernel, orbitals),
        out_shape=jax.ShapeDtypeStruct((2, rows, span), BF16),
        scratch_shapes=[
            pltpu.VMEM((pairs, orbitals * (2 * orbitals + 1), aux), F32),
            pltpu.VMEM((pairs, 2 * flat, aux), BF16),
            pltpu.VMEM((flat, pairs * aux), BF16),
            pltpu.VMEM((pairs * aux, flat), BF16),
        ],
        compiler_params=pltpu.CompilerParams(vmem_limit_bytes=42 * MIB),
        name="self_energy",
    )(green, fit, turned)


def collide_kernel(offsets, row_devices, place_ref, near_ref, far_ref, *refs):
    pieces, (keep_ref, send_ref, sums) = refs[:-3], refs[-3:]
    row, col = place_ref[0], place_ref[1]
    _, _, rows, span = near_ref.shape
    half = near_ref.shape[0]
    ratio = row_devices // len(pieces)
    blocks = []
    for b in range(2 * half):
        ref, at = (near_ref, b) if b < half else (far_ref, b - half)
        blocks.append(jnp.concatenate([ref[at, c] for c in range(2)], axis=0))
    for s, piece in enumerate(pieces):
        acc = None
        for b, offset in enumerate(offsets):
            at = pl.ds(pl.multiple_of((col ^ offset) * span, span), span)
            h = jnp.concatenate([piece[c, at, :] for c in range(2)], axis=1)
            r = dot(blocks[b], h)
            acc = r if acc is None else acc + r
        width = ratio * span
        real = acc[:rows, :width] - acc[rows:, width:]
        imag = acc[:rows, width:] + acc[rows:, :width]
        for rho in range(ratio):
            t = ((col ^ s) * ratio + rho) ^ row
            sums[t, 0] = real[:, rho * span : (rho + 1) * span]
            sums[t, 1] = imag[:, rho * span : (rho + 1) * span]
    for t in range(row_devices):
        if t & 1:
            send_ref[t // 2] = sums[t].astype(BF16)
        else:
            keep_ref[t // 2] = sums[t]


def collide(place, near, far, pieces, offsets, row_devices):
    _, _, rows, span = near.shape
    shape = (row_devices // 2, 2, rows, span)
    return pl.pallas_call(
        functools.partial(collide_kernel, offsets, row_devices),
        out_shape=(jax.ShapeDtypeStruct(shape, F32), jax.ShapeDtypeStruct(shape, BF16)),
        in_specs=[pl.BlockSpec(memory_space=pltpu.SMEM)]
        + [pl.BlockSpec(memory_space=pltpu.VMEM)] * (2 + len(pieces)),
        scratch_shapes=[pltpu.VMEM((row_devices, 2, rows, span), F32)],
        compiler_params=pltpu.CompilerParams(vmem_limit_bytes=32 * MIB),
        name="collide",
    )(place, near, far, *pieces)


def swap(x, axis, step):
    size = lax.axis_size(axis)
    return lax.ppermute(x, axis, [(d, d ^ step) for d in range(size)])


def bits(size):
    return [1 << b for b in range(size.bit_length() - 1)]


def local(green_start, fit, history):
    orbitals = math.isqrt(fit.shape[1])
    _, rows, span = green_start.shape
    row_devices = lax.axis_size("row")
    col_devices = lax.axis_size("col")
    ratio = row_devices // col_devices
    row, col = lax.axis_index("row"), lax.axis_index("col")
    place = jnp.stack([row, col]).astype(jnp.int32)

    depth = history.shape[1]
    split = history.reshape(2, depth, ratio, col_devices, span)
    pieces = []
    for s in range(col_devices):
        piece = lax.dynamic_index_in_dim(split, col ^ s, axis=3, keepdims=False)
        piece = piece.reshape(2, depth, ratio * span)
        pieces.append(swap(piece, "col", s) if s else piece)

    turned = turn(fit, orbitals)
    green = green_start
    for _ in range(ITERS):
        sigma = energy(green, fit, turned, orbitals)
        near, offsets = sigma[None], [0]
        far = None
        for step in reversed(bits(col_devices)):
            if far is not None:
                near = jnp.concatenate([near, far], axis=0)
            far = swap(near, "col", step)
            offsets = offsets + [o ^ step for o in offsets]
        keep, send = collide(place, near, far, pieces, offsets, row_devices)
        for step in bits(row_devices):
            if step > 1:
                send = keep[1::2].astype(BF16)
                keep = keep[0::2]
            keep = keep + swap(send, "row", step).astype(F32)
        green = green_start + keep[0]
    return green


def solution(mesh):
    in_specs = (P("groups", None, ("row", "col")), P("groups", None), P("groups", "row", "col"))
    out_specs = P("groups", None, ("row", "col"))
    return jax.shard_map(local, mesh=mesh, in_specs=in_specs, out_specs=out_specs, check_vma=False)
```

```python
import functools
import math

import jax
import jax.numpy as jnp
from jax import lax
from jax.experimental import pallas as pl
from jax.experimental.pallas import tpu as pltpu
from jax.sharding import PartitionSpec as P

ITERS = 2
BF16 = jnp.bfloat16
F32 = jnp.float32
LANES = 128
MIB = 2**20


def dot(a, b):
    return jnp.dot(a, b, preferred_element_type=F32)


def dot_nt(a, b):
    return lax.dot_general(a, b, (((1,), (1,)), ((), ())), preferred_element_type=F32)


def split_kernel(span, place_ref, history_ref, *refs):
    pieces, sems = refs[:-1], refs[-1]
    ratio = pieces[0].shape[2] // span
    copies = []
    for s, piece in enumerate(pieces):
        for rho in range(ratio):
            at = pl.multiple_of((rho * len(pieces) + (place_ref[1] ^ s)) * span, span)
            copies.append(
                pltpu.make_async_copy(
                    history_ref.at[:, :, pl.ds(at, span)],
                    piece.at[:, :, pl.ds(rho * span, span)],
                    sems.at[s, rho],
                )
            )
    for copy in copies:
        copy.start()
    for copy in copies:
        copy.wait()


def split_history(place, history, span, col_devices):
    _, depth, width = history.shape
    ratio = width // span // col_devices
    piece = jax.ShapeDtypeStruct((2, depth, ratio * span), BF16)
    return pl.pallas_call(
        functools.partial(split_kernel, span),
        out_shape=[piece] * col_devices,
        in_specs=[pl.BlockSpec(memory_space=pltpu.SMEM), pl.BlockSpec(memory_space=pltpu.VMEM)],
        out_specs=[pl.BlockSpec(memory_space=pl.ANY)] * col_devices,
        scratch_shapes=[pltpu.SemaphoreType.DMA((col_devices, ratio))],
        compiler_params=pltpu.CompilerParams(vmem_limit_bytes=16 * MIB),
        name="split_history",
    )(place, history)


def energy_kernel(orbitals, turn, green_ref, fit_ref, *refs):
    if turn:
        out_ref, turned_ref, spread, left, under, screened, wide = refs
    else:
        turned_ref, out_ref, spread, left, under, screened = refs
    aux, flat = fit_ref.shape
    times = green_ref.shape[2] // orbitals
    new = green_ref.shape[1] // orbitals
    pairs = new * times
    pitch = 2 * orbitals + 1
    per = LANES // orbitals
    flipped = [
        [green_ref[c, a * orbitals : (a + 1) * orbitals, :].T.astype(BF16) for c in range(2)]
        for a in range(new)
    ]
    lhs = jnp.concatenate([flipped[a][c] for a in range(new) for c in range(2)], axis=0)
    zero = jnp.zeros_like(lhs)
    both = [
        jnp.concatenate([lhs if q == h else zero for q in range(per)], axis=1) for h in range(per)
    ]
    for i in range(0, orbitals, 2 * per):
        if turn:
            for t in range(i // per, i // per + 2):
                at = slice(t * LANES, (t + 1) * LANES)
                wide[at, :] = fit_ref[:, at].astype(F32).T
        w = jnp.concatenate(
            [fit_ref[:, (i + per * g) * orbitals : (i + per * (g + 1)) * orbitals] for g in range(2)],
            axis=0,
        )
        for h in range(per):
            res = dot_nt(both[h], w)
            for g in range(2):
                for a in range(new):
                    for c in range(2):
                        for k in range(times):
                            r = ((a * 2 + c) * times + k) * orbitals
                            spread[
                                a * times + k,
                                pl.ds(c * orbitals + i + per * g + h, orbitals, stride=pitch),
                                :,
                            ] = res[r : r + orbitals, g * aux : (g + 1) * aux]
    around = [jnp.concatenate(flipped[a], axis=1) for a in range(new)]
    rows = 2 * orbitals
    for m in range(0, orbitals, 2):
        if turn and m % per == 0:
            x = [wide[pl.ds(m + h, orbitals, stride=orbitals), :] for h in range(per)]
            at = slice(m * orbitals, (m + per) * orbitals)
            turned_ref[:, at] = jnp.concatenate(x, axis=0).T.astype(BF16)
        for n in range(pairs):
            a, k = divmod(n, times)
            x = [spread[n, pl.ds((m + h) * pitch, rows), :].astype(BF16) for h in range(2)]
            for h in range(2):
                left[n, (m + h) * rows : (m + h + 1) * rows, :] = x[h]
            r = dot(around[a][k * orbitals : (k + 1) * orbitals], jnp.concatenate(x, axis=1))
            for h in range(2):
                under[(m + h) * orbitals : (m + h + 1) * orbitals, n * aux : (n + 1) * aux] = r[
                    :, h * aux : (h + 1) * aux
                ].astype(BF16)
    pi = dot(turned_ref[...], under[...]) * (1.0 / orbitals)
    bubble = jnp.concatenate([pi[:, n * aux : (n + 1) * aux].T for n in range(pairs)], axis=0)
    screened[...] = dot(bubble.astype(BF16), fit_ref[...]).astype(BF16)
    scale = (aux * orbitals) ** -0.5
    accs = [jnp.zeros((rows, orbitals), F32) for _ in range(pairs)]
    for m in range(0, orbitals, 2):
        for n in range(pairs):
            a = jnp.concatenate(
                [left[n, (m + h) * rows : (m + h + 1) * rows, :] for h in range(2)], axis=1
            )
            w = screened[n * aux : (n + 1) * aux, m * orbitals : (m + 2) * orbitals]
            b = jnp.concatenate([w[:, :orbitals], w[:, orbitals:]], axis=0)
            accs[n] = accs[n] + dot(a, b)
    for n in range(pairs):
        a, k = divmod(n, times)
        block = (accs[n] * scale).astype(BF16)
        for c in range(2):
            out_ref[
                c, a * orbitals : (a + 1) * orbitals, k * orbitals : (k + 1) * orbitals
            ] = block[c * orbitals : (c + 1) * orbitals]


def energy(green, fit, turned, orbitals):
    aux, flat = fit.shape
    _, rows, span = green.shape
    pairs = rows // orbitals * (span // orbitals)
    turn = turned is None
    out_shape = jax.ShapeDtypeStruct((2, rows, span), BF16)
    scratch = [
        pltpu.VMEM((pairs, orbitals * (2 * orbitals + 1), aux), F32),
        pltpu.VMEM((pairs, 2 * flat, aux), BF16),
        pltpu.VMEM((flat, pairs * aux), BF16),
        pltpu.VMEM((pairs * aux, flat), BF16),
    ]
    return pl.pallas_call(
        functools.partial(energy_kernel, orbitals, turn),
        out_shape=[out_shape, jax.ShapeDtypeStruct((aux, flat), BF16)] if turn else out_shape,
        scratch_shapes=scratch + [pltpu.VMEM((flat, aux), F32)] * turn,
        compiler_params=pltpu.CompilerParams(vmem_limit_bytes=44 * MIB),
        name="self_energy",
    )(*((green, fit) if turn else (green, fit, turned)))


def collide_kernel(offsets, row_devices, place_ref, near_ref, far_ref, *refs):
    pieces, keep_ref, sends, sums = refs[: -row_devices - 1], refs[-row_devices - 1], refs[-row_devices:-1], refs[-1]
    row, col = place_ref[0], place_ref[1]
    _, _, rows, span = near_ref.shape
    half = near_ref.shape[0]
    ratio = row_devices // len(pieces)
    blocks = []
    for b in range(2 * half):
        ref, at = (near_ref, b) if b < half else (far_ref, b - half)
        blocks.append(jnp.concatenate([ref[at, c] for c in range(2)], axis=0))
    for s, piece in enumerate(pieces):
        acc = None
        for b, offset in enumerate(offsets):
            at = pl.ds(pl.multiple_of((col ^ offset) * span, span), span)
            h = jnp.concatenate([piece[c, at, :] for c in range(2)], axis=1)
            r = dot(blocks[b], h)
            acc = r if acc is None else acc + r
        width = ratio * span
        real = acc[:rows, :width] - acc[rows:, width:]
        imag = acc[:rows, width:] + acc[rows:, :width]
        for rho in range(ratio):
            t = ((col ^ s) * ratio + rho) ^ row
            sums[t, 0] = real[:, rho * span : (rho + 1) * span]
            sums[t, 1] = imag[:, rho * span : (rho + 1) * span]
    keep_ref[...] = sums[0]
    for t in range(1, row_devices):
        sends[t - 1][...] = sums[t].astype(BF16)


def collide(place, near, far, pieces, offsets, row_devices):
    _, _, rows, span = near.shape
    shape = (2, rows, span)
    return pl.pallas_call(
        functools.partial(collide_kernel, offsets, row_devices),
        out_shape=[jax.ShapeDtypeStruct(shape, F32)]
        + [jax.ShapeDtypeStruct(shape, BF16)] * (row_devices - 1),
        in_specs=[pl.BlockSpec(memory_space=pltpu.SMEM)]
        + [pl.BlockSpec(memory_space=pltpu.VMEM)] * (2 + len(pieces)),
        scratch_shapes=[pltpu.VMEM((row_devices, 2, rows, span), F32)],
        compiler_params=pltpu.CompilerParams(vmem_limit_bytes=32 * MIB),
        name="collide",
    )(place, near, far, *pieces)


def swap(x, axis, step):
    size = lax.axis_size(axis)
    return lax.ppermute(x, axis, [(d, d ^ step) for d in range(size)])


def bits(size):
    return [1 << b for b in range(size.bit_length() - 1)]


def local(green_start, fit, history):
    orbitals = math.isqrt(fit.shape[1])
    _, rows, span = green_start.shape
    row_devices = lax.axis_size("row")
    col_devices = lax.axis_size("col")
    place = jnp.stack([lax.axis_index("row"), lax.axis_index("col")]).astype(jnp.int32)

    pieces = split_history(place, history, span, col_devices)
    pieces = [swap(piece, "col", s) if s else piece for s, piece in enumerate(pieces)]

    green, turned = green_start, None
    for _ in range(ITERS):
        if turned is None:
            sigma, turned = energy(green, fit, None, orbitals)
            sigma, pieces = lax.optimization_barrier((sigma, pieces))
        else:
            sigma = energy(green, fit, turned, orbitals)
        near, offsets = sigma[None], [0]
        far = None
        for step in reversed(bits(col_devices)):
            if far is not None:
                near = jnp.concatenate([near, far], axis=0)
            far = swap(near, "col", step)
            offsets = offsets + [o ^ step for o in offsets]
        keep, *sends = collide(place, near, far, pieces, offsets, row_devices)
        green = green_start + keep
        for step in sorted(range(1, row_devices), key=lambda t: -(t ^ 1)):
            green = green + swap(sends[step - 1], "row", step).astype(F32)
    return green


def solution(mesh):
    in_specs = (P("groups", None, ("row", "col")), P("groups", None), P("groups", "row", "col"))
    out_specs = P("groups", None, ("row", "col"))
    return jax.shard_map(local, mesh=mesh, in_specs=in_specs, out_specs=out_specs, check_vma=False)
```

```python
import functools
import math

import jax
import jax.numpy as jnp
from jax import lax
from jax.experimental import pallas as pl
from jax.experimental.pallas import tpu as pltpu
from jax.sharding import PartitionSpec as P

ITERS = 2
BF16 = jnp.bfloat16
F32 = jnp.float32
LANES = 128
MIB = 2**20


def dot(a, b):
    return jnp.dot(a, b, preferred_element_type=F32)


def dot_nt(a, b):
    return lax.dot_general(a, b, (((1,), (1,)), ((), ())), preferred_element_type=F32)


def split_kernel(place_ref, green_ref, history_ref, green_out_ref, *refs):
    groups, sems = refs[:-1], refs[-1]
    columns = 1 << (len(groups) - 1)
    span = green_ref.shape[2]
    ratio = groups[0].shape[3] // span
    copies = [pltpu.make_async_copy(green_ref, green_out_ref, sems.at[columns, 0])]
    for d in range(columns):
        piece = groups[d.bit_length()].at[d - (1 << d.bit_length() >> 1)]
        for rho in range(ratio):
            at = pl.multiple_of((rho * columns + (place_ref[1] ^ d)) * span, span)
            copies.append(
                pltpu.make_async_copy(
                    history_ref.at[:, :, pl.ds(at, span)],
                    piece.at[:, :, pl.ds(rho * span, span)],
                    sems.at[d, rho],
                )
            )
    for copy in copies:
        copy.start()
    for copy in copies:
        copy.wait()


def split_history(place, green, history, col_devices):
    _, depth, width = history.shape
    span = green.shape[2]
    ratio = width // span // col_devices
    anywhere = pl.BlockSpec(memory_space=pl.ANY)
    sizes = [1, *bits(col_devices)]
    return pl.pallas_call(
        split_kernel,
        out_shape=[jax.ShapeDtypeStruct(green.shape, F32)]
        + [jax.ShapeDtypeStruct((n, 2, depth, ratio * span), BF16) for n in sizes],
        in_specs=[pl.BlockSpec(memory_space=pltpu.SMEM), anywhere, anywhere],
        out_specs=[anywhere] * (1 + len(sizes)),
        scratch_shapes=[pltpu.SemaphoreType.DMA((col_devices + 1, ratio))],
        compiler_params=pltpu.CompilerParams(vmem_limit_bytes=16 * MIB),
        name="split_history",
    )(
        place,
        pltpu.with_memory_space_constraint(green, pltpu.HBM),
        pltpu.with_memory_space_constraint(history, pltpu.HBM),
    )


def energy_kernel(orbitals, turn, green_ref, fit_ref, *refs):
    if turn:
        out_ref, turned_ref, tall_ref, spread, left, under, wide = refs
    else:
        turned_ref, tall_ref, out_ref, spread, left, under = refs
    aux, flat = fit_ref.shape
    times = green_ref.shape[2] // orbitals
    new = green_ref.shape[1] // orbitals
    pairs = new * times
    pitch = 2 * orbitals + 1
    per = LANES // orbitals
    flipped = [
        [green_ref[c, a * orbitals : (a + 1) * orbitals, :].T.astype(BF16) for c in range(2)]
        for a in range(new)
    ]
    lhs = jnp.concatenate([flipped[a][c] for a in range(new) for c in range(2)], axis=0)
    zero = jnp.zeros_like(lhs)
    both = [
        jnp.concatenate([lhs if q == h else zero for q in range(per)], axis=1) for h in range(per)
    ]
    for i in range(0, orbitals, 2 * per):
        if turn:
            for t in range(i // per, i // per + 2):
                at = slice(t * LANES, (t + 1) * LANES)
                wide[at, :] = fit_ref[:, at].astype(F32).T
                tall_ref[at, :] = wide[at, :].astype(BF16)
        w = jnp.concatenate(
            [fit_ref[:, (i + per * g) * orbitals : (i + per * (g + 1)) * orbitals] for g in range(2)],
            axis=0,
        )
        for h in range(per):
            res = dot_nt(both[h], w)
            for g in range(2):
                for a in range(new):
                    for c in range(2):
                        for k in range(times):
                            r = ((a * 2 + c) * times + k) * orbitals
                            spread[
                                a * times + k,
                                pl.ds(c * orbitals + i + per * g + h, orbitals, stride=pitch),
                                :,
                            ] = res[r : r + orbitals, g * aux : (g + 1) * aux]
    around = [jnp.concatenate(flipped[a], axis=1) for a in range(new)]
    rows = 2 * orbitals
    group = 2
    for m in range(0, orbitals, 2):
        if turn and m % per == 0:
            x = [wide[pl.ds(m + h, orbitals, stride=orbitals), :] for h in range(per)]
            at = slice(m * orbitals, (m + per) * orbitals)
            turned_ref[:, at] = jnp.concatenate(x, axis=0).T.astype(BF16)
        for n in range(pairs):
            a, k = divmod(n, times)
            x = [spread[n, pl.ds((m + h) * pitch, rows), :].astype(BF16) for h in range(2)]
            for h in range(2):
                left[n, (m + h) * rows : (m + h + 1) * rows, :] = x[h]
            r = dot(around[a][k * orbitals : (k + 1) * orbitals], jnp.concatenate(x, axis=1))
            for h in range(2):
                under[(m + h) * orbitals : (m + h + 1) * orbitals, n * aux : (n + 1) * aux] = r[
                    :, h * aux : (h + 1) * aux
                ].astype(BF16)
    bubble = dot(turned_ref[...], under[...]) * (1.0 / orbitals)
    screened = under
    screened[...] = dot(tall_ref[...], bubble.astype(BF16)).astype(BF16)
    scale = (aux * orbitals) ** -0.5
    for n in range(pairs):
        acc = jnp.zeros((orbitals, rows), F32)
        for l in range(0, orbitals, group):
            a = [
                screened[(l + h) * orbitals : (l + h + 1) * orbitals, n * aux : (n + 1) * aux]
                for h in range(group)
            ]
            b = [left[n, (l + h) * rows : (l + h + 1) * rows, :] for h in range(group)]
            acc = acc + dot_nt(jnp.concatenate(a, axis=1), jnp.concatenate(b, axis=1))
        block = (acc * scale).T.astype(BF16)
        a, k = divmod(n, times)
        for c in range(2):
            out_ref[
                c, a * orbitals : (a + 1) * orbitals, k * orbitals : (k + 1) * orbitals
            ] = block[c * orbitals : (c + 1) * orbitals]


def energy(green, fit, turned, orbitals):
    aux, flat = fit.shape
    _, rows, span = green.shape
    pairs = rows // orbitals * (span // orbitals)
    turn = turned is None
    out_shape = jax.ShapeDtypeStruct((2, rows, span), BF16)
    forms = [jax.ShapeDtypeStruct((aux, flat), BF16), jax.ShapeDtypeStruct((flat, aux), BF16)]
    scratch = [
        pltpu.VMEM((pairs, orbitals * (2 * orbitals + 1), aux), F32),
        pltpu.VMEM((pairs, 2 * flat, aux), BF16),
        pltpu.VMEM((flat, pairs * aux), BF16),
    ]
    return pl.pallas_call(
        functools.partial(energy_kernel, orbitals, turn),
        out_shape=[out_shape, *forms] if turn else out_shape,
        scratch_shapes=scratch + [pltpu.VMEM((flat, aux), F32)] * turn,
        compiler_params=pltpu.CompilerParams(vmem_limit_bytes=36 * MIB),
        name="self_energy",
    )(green, fit, *(() if turn else turned))


def collide_kernel(offsets, row_devices, place_ref, near_ref, far_ref, *refs):
    pieces, keep_ref, sends, sums = refs[: -row_devices - 1], refs[-row_devices - 1], refs[-row_devices:-1], refs[-1]
    row, col = place_ref[0], place_ref[1]
    _, _, rows, span = near_ref.shape
    half = near_ref.shape[0]
    ratio = row_devices // len(pieces)
    blocks = []
    for b in range(2 * half):
        ref, at = (near_ref, b) if b < half else (far_ref, b - half)
        blocks.append(jnp.concatenate([ref[at, c] for c in range(2)], axis=0))
    stacked = jnp.concatenate(blocks, axis=1)
    for s, piece in enumerate(pieces):
        depth = []
        for offset in offsets:
            at = pl.ds(pl.multiple_of((col ^ offset) * span, span), span)
            depth.append(jnp.concatenate([piece[0, c, at, :] for c in range(2)], axis=1))
        acc = dot(stacked, jnp.concatenate(depth, axis=0))
        width = ratio * span
        real = acc[:rows, :width] - acc[rows:, width:]
        imag = acc[:rows, width:] + acc[rows:, :width]
        for rho in range(ratio):
            t = ((col ^ s) * ratio + rho) ^ row
            sums[t, 0] = real[:, rho * span : (rho + 1) * span]
            sums[t, 1] = imag[:, rho * span : (rho + 1) * span]
    keep_ref[...] = sums[0]
    for t in range(1, row_devices):
        sends[t - 1][...] = sums[t].astype(BF16)


def collide(place, near, far, pieces, offsets, row_devices):
    _, _, rows, span = near.shape
    shape = (2, rows, span)
    return pl.pallas_call(
        functools.partial(collide_kernel, offsets, row_devices),
        grid=(1,),
        out_shape=[jax.ShapeDtypeStruct(shape, F32)]
        + [jax.ShapeDtypeStruct(shape, BF16)] * (row_devices - 1),
        in_specs=[pl.BlockSpec(memory_space=pltpu.SMEM)]
        + [pl.BlockSpec(memory_space=pltpu.VMEM)] * 2
        + [pl.BlockSpec((1, *piece.shape[1:]), lambda _: (0, 0, 0, 0)) for piece in pieces],
        scratch_shapes=[pltpu.VMEM((row_devices, 2, rows, span), F32)],
        compiler_params=pltpu.CompilerParams(vmem_limit_bytes=32 * MIB),
        name="collide",
    )(place, near, far, *pieces)


def swap(x, axis, step):
    size = lax.axis_size(axis)
    return lax.ppermute(x, axis, [(d, d ^ step) for d in range(size)])


def bits(size):
    return [1 << b for b in range(size.bit_length() - 1)]


def local(green_start, fit, history):
    orbitals = math.isqrt(fit.shape[1])
    row_devices = lax.axis_size("row")
    col_devices = lax.axis_size("col")
    place = jnp.stack([lax.axis_index("row"), lax.axis_index("col")]).astype(jnp.int32)

    green_start, kept, *groups = split_history(place, green_start, history, col_devices)
    held = {0: kept}

    def pass_on(step):
        for offset, array in list(held.items()):
            if array.shape[0] > step:
                held[offset ^ step] = swap(array[step : 2 * step], "col", step)
        held[step] = swap(groups.pop(), "col", step)

    steps = bits(col_devices)[::-1]
    pass_on(steps[0])
    green, turned = green_start, None
    for _ in range(ITERS):
        if turned is None:
            sigma, *turned = energy(green, fit, None, orbitals)
            sigma, held = lax.optimization_barrier((sigma, held))
            for step in steps[1:]:
                pass_on(step)
            pieces = [held[offset] for offset in range(col_devices)]
        else:
            sigma = energy(green, fit, turned, orbitals)
        near, offsets = sigma[None], [0]
        far = None
        for step in steps:
            if far is not None:
                near = jnp.concatenate([near, far], axis=0)
            far = swap(near, "col", step)
            offsets = offsets + [o ^ step for o in offsets]
        keep, *sends = collide(place, near, far, pieces, offsets, row_devices)
        green = green_start + keep
        for step in sorted(range(1, row_devices), key=lambda t: -(t ^ 1)):
            green = green + swap(sends[step - 1], "row", step).astype(F32)
    return green


def solution(mesh):
    in_specs = (P("groups", None, ("row", "col")), P("groups", None), P("groups", "row", "col"))
    out_specs = P("groups", None, ("row", "col"))
    return jax.shard_map(local, mesh=mesh, in_specs=in_specs, out_specs=out_specs, check_vma=False)
```

```python
import functools
import math

import jax
import jax.numpy as jnp
from jax import lax
from jax.experimental import pallas as pl
from jax.experimental.pallas import tpu as pltpu
from jax.sharding import PartitionSpec as P

ITERS = 2
BF16 = jnp.bfloat16
F32 = jnp.float32
LANES = 128
MIB = 2**20


def dot(a, b):
    return jnp.dot(a, b, preferred_element_type=F32)


def dot_nt(a, b):
    return lax.dot_general(a, b, (((1,), (1,)), ((), ())), preferred_element_type=F32)


def split_kernel(place_ref, green_ref, history_ref, green_out_ref, *refs):
    groups, sems = refs[:-1], refs[-1]
    columns = 1 << (len(groups) - 1)
    span = green_ref.shape[2]
    ratio = groups[0].shape[3] // span
    copies = [pltpu.make_async_copy(green_ref, green_out_ref, sems.at[columns, 0])]
    for d in range(columns):
        piece = groups[d.bit_length()].at[d - (1 << d.bit_length() >> 1)]
        for rho in range(ratio):
            at = pl.multiple_of((rho * columns + (place_ref[1] ^ d)) * span, span)
            copies.append(
                pltpu.make_async_copy(
                    history_ref.at[:, :, pl.ds(at, span)],
                    piece.at[:, :, pl.ds(rho * span, span)],
                    sems.at[d, rho],
                )
            )
    for copy in copies:
        copy.start()
    for copy in copies:
        copy.wait()


def split_history(place, green, history, col_devices):
    _, depth, width = history.shape
    span = green.shape[2]
    ratio = width // span // col_devices
    anywhere = pl.BlockSpec(memory_space=pl.ANY)
    sizes = [1, *bits(col_devices)]
    return pl.pallas_call(
        split_kernel,
        out_shape=[jax.ShapeDtypeStruct(green.shape, F32)]
        + [jax.ShapeDtypeStruct((n, 2, depth, ratio * span), BF16) for n in sizes],
        in_specs=[pl.BlockSpec(memory_space=pltpu.SMEM), anywhere, anywhere],
        out_specs=[anywhere] * (1 + len(sizes)),
        scratch_shapes=[pltpu.SemaphoreType.DMA((col_devices + 1, ratio))],
        compiler_params=pltpu.CompilerParams(vmem_limit_bytes=16 * MIB),
        name="split_history",
    )(
        place,
        pltpu.with_memory_space_constraint(green, pltpu.HBM),
        pltpu.with_memory_space_constraint(history, pltpu.HBM),
    )


def energy_kernel(orbitals, turn, green_ref, fit_ref, *refs):
    if turn:
        out_ref, turned_ref, tall_ref, spread, left, under, wide = refs
    else:
        turned_ref, tall_ref, out_ref, spread, left, under = refs
    aux, flat = fit_ref.shape
    times = green_ref.shape[2] // orbitals
    new = green_ref.shape[1] // orbitals
    pairs = new * times
    pitch = 2 * orbitals + 1
    per = LANES // orbitals
    flipped = [
        [green_ref[c, a * orbitals : (a + 1) * orbitals, :].T.astype(BF16) for c in range(2)]
        for a in range(new)
    ]
    lhs = jnp.concatenate([flipped[a][c] for a in range(new) for c in range(2)], axis=0)
    zero = jnp.zeros_like(lhs)
    both = [
        jnp.concatenate([lhs if q == h else zero for q in range(per)], axis=1) for h in range(per)
    ]
    for i in range(0, orbitals, 2 * per):
        if turn:
            for t in range(i // per, i // per + 2):
                at = slice(t * LANES, (t + 1) * LANES)
                wide[at, :] = fit_ref[:, at].astype(F32).T
                tall_ref[at, :] = wide[at, :].astype(BF16)
        w = jnp.concatenate(
            [fit_ref[:, (i + per * g) * orbitals : (i + per * (g + 1)) * orbitals] for g in range(2)],
            axis=0,
        )
        for h in range(per):
            res = dot_nt(both[h], w)
            for g in range(2):
                for a in range(new):
                    for c in range(2):
                        for k in range(times):
                            r = ((a * 2 + c) * times + k) * orbitals
                            spread[
                                a * times + k,
                                pl.ds(c * orbitals + i + per * g + h, orbitals, stride=pitch),
                                :,
                            ] = res[r : r + orbitals, g * aux : (g + 1) * aux]
    around = [jnp.concatenate(flipped[a], axis=1) for a in range(new)]
    rows = 2 * orbitals
    group = 2
    for m in range(0, orbitals, 2):
        if turn and m % per == 0:
            x = [wide[pl.ds(m + h, orbitals, stride=orbitals), :] for h in range(per)]
            at = slice(m * orbitals, (m + per) * orbitals)
            turned_ref[:, at] = jnp.concatenate(x, axis=0).T.astype(BF16)
        for n in range(pairs):
            a, k = divmod(n, times)
            x = [spread[n, pl.ds((m + h) * pitch, rows), :].astype(BF16) for h in range(2)]
            for h in range(2):
                left[n, (m + h) * rows : (m + h + 1) * rows, :] = x[h]
            r = dot(around[a][k * orbitals : (k + 1) * orbitals], jnp.concatenate(x, axis=1))
            for h in range(2):
                under[(m + h) * orbitals : (m + h + 1) * orbitals, n * aux : (n + 1) * aux] = r[
                    :, h * aux : (h + 1) * aux
                ].astype(BF16)
    bubble = dot(turned_ref[...], under[...]) * (1.0 / orbitals)
    screened = under
    screened[...] = dot(tall_ref[...], bubble.astype(BF16)).astype(BF16)
    scale = (aux * orbitals) ** -0.5
    for n in range(pairs):
        acc = jnp.zeros((orbitals, rows), F32)
        for l in range(0, orbitals, group):
            a = [
                screened[(l + h) * orbitals : (l + h + 1) * orbitals, n * aux : (n + 1) * aux]
                for h in range(group)
            ]
            b = [left[n, (l + h) * rows : (l + h + 1) * rows, :] for h in range(group)]
            acc = acc + dot_nt(jnp.concatenate(a, axis=1), jnp.concatenate(b, axis=1))
        block = (acc * scale).T.astype(BF16)
        a, k = divmod(n, times)
        for c in range(2):
            out_ref[
                c, a * orbitals : (a + 1) * orbitals, k * orbitals : (k + 1) * orbitals
            ] = block[c * orbitals : (c + 1) * orbitals]


def energy(green, fit, turned, orbitals):
    aux, flat = fit.shape
    _, rows, span = green.shape
    pairs = rows // orbitals * (span // orbitals)
    turn = turned is None
    out_shape = jax.ShapeDtypeStruct((2, rows, span), BF16)
    forms = [jax.ShapeDtypeStruct((aux, flat), BF16), jax.ShapeDtypeStruct((flat, aux), BF16)]
    scratch = [
        pltpu.VMEM((pairs, orbitals * (2 * orbitals + 1), aux), F32),
        pltpu.VMEM((pairs, 2 * flat, aux), BF16),
        pltpu.VMEM((flat, pairs * aux), BF16),
    ]
    return pl.pallas_call(
        functools.partial(energy_kernel, orbitals, turn),
        out_shape=[out_shape, *forms] if turn else out_shape,
        scratch_shapes=scratch + [pltpu.VMEM((flat, aux), F32)] * turn,
        compiler_params=pltpu.CompilerParams(vmem_limit_bytes=36 * MIB),
        name="self_energy",
    )(green, fit, *(() if turn else turned))


def collide_kernel(offsets, row_devices, place_ref, near_ref, far_ref, *refs):
    pieces, keep_ref, sends, sums = refs[: -row_devices - 1], refs[-row_devices - 1], refs[-row_devices:-1], refs[-1]
    row, col = place_ref[0], place_ref[1]
    _, _, rows, span = near_ref.shape
    half = near_ref.shape[0]
    ratio = row_devices // len(pieces)
    blocks = []
    for b in range(2 * half):
        ref, at = (near_ref, b) if b < half else (far_ref, b - half)
        blocks.append(jnp.concatenate([ref[at, c] for c in range(2)], axis=0))
    stacked = jnp.concatenate(blocks, axis=1)
    for s, piece in enumerate(pieces):
        depth = []
        for offset in offsets:
            at = pl.ds(pl.multiple_of((col ^ offset) * span, span), span)
            depth.append(jnp.concatenate([piece[0, c, at, :] for c in range(2)], axis=1))
        acc = dot(stacked, jnp.concatenate(depth, axis=0))
        width = ratio * span
        real = acc[:rows, :width] - acc[rows:, width:]
        imag = acc[:rows, width:] + acc[rows:, :width]
        for rho in range(ratio):
            t = ((col ^ s) * ratio + rho) ^ row
            sums[t, 0] = real[:, rho * span : (rho + 1) * span]
            sums[t, 1] = imag[:, rho * span : (rho + 1) * span]
    keep_ref[...] = sums[0]
    for t in range(1, row_devices):
        sends[t - 1][...] = sums[t].astype(BF16)


def collide(place, near, far, pieces, offsets, row_devices):
    _, _, rows, span = near.shape
    shape = (2, rows, span)
    return pl.pallas_call(
        functools.partial(collide_kernel, offsets, row_devices),
        grid=(1,),
        out_shape=[jax.ShapeDtypeStruct(shape, F32)]
        + [jax.ShapeDtypeStruct(shape, BF16)] * (row_devices - 1),
        in_specs=[pl.BlockSpec(memory_space=pltpu.SMEM)]
        + [pl.BlockSpec(memory_space=pltpu.VMEM)] * 2
        + [pl.BlockSpec((1, *piece.shape[1:]), lambda _: (0, 0, 0, 0)) for piece in pieces],
        scratch_shapes=[pltpu.VMEM((row_devices, 2, rows, span), F32)],
        compiler_params=pltpu.CompilerParams(vmem_limit_bytes=32 * MIB),
        name="collide",
    )(place, near, far, *pieces)


def swap(x, axis, step):
    size = lax.axis_size(axis)
    return lax.ppermute(x, axis, [(d, d ^ step) for d in range(size)])


def bits(size):
    return [1 << b for b in range(size.bit_length() - 1)]


def local(green_start, fit, history):
    orbitals = math.isqrt(fit.shape[1])
    row_devices = lax.axis_size("row")
    col_devices = lax.axis_size("col")
    place = jnp.stack([lax.axis_index("row"), lax.axis_index("col")]).astype(jnp.int32)

    green_start, kept, *groups = split_history(place, green_start, history, col_devices)
    held = {0: kept}

    def pass_on(step):
        for offset, array in list(held.items()):
            if array.shape[0] > step:
                held[offset ^ step] = swap(array[step : 2 * step], "col", step)
        held[step] = swap(groups.pop(), "col", step)

    steps = bits(col_devices)[::-1]
    pass_on(steps[0])
    green, turned = green_start, None
    for _ in range(ITERS):
        if turned is None:
            sigma, *turned = energy(green, fit, None, orbitals)
        else:
            sigma = energy(green, fit, turned, orbitals)
        near, offsets = sigma[None], [0]
        far = None
        for step in steps:
            if far is not None:
                near = jnp.concatenate([near, far], axis=0)
            far = swap(near, "col", step)
            if held:
                far, held = lax.optimization_barrier((far, held))
                for later in steps[1:]:
                    pass_on(later)
                pieces, held = [held[offset] for offset in range(col_devices)], None
            offsets = offsets + [o ^ step for o in offsets]
        keep, *sends = collide(place, near, far, pieces, offsets, row_devices)
        green = green_start + keep
        for step in sorted(range(1, row_devices), key=lambda t: -(t ^ 1)):
            green = green + swap(sends[step - 1], "row", step).astype(F32)
    return green


def solution(mesh):
    in_specs = (P("groups", None, ("row", "col")), P("groups", None), P("groups", "row", "col"))
    out_specs = P("groups", None, ("row", "col"))
    return jax.shard_map(local, mesh=mesh, in_specs=in_specs, out_specs=out_specs, check_vma=False)
```

```python
import functools
import math

import jax
import jax.numpy as jnp
from jax import lax
from jax.experimental import pallas as pl
from jax.experimental.pallas import tpu as pltpu
from jax.sharding import PartitionSpec as P

ITERS = 2
BF16 = jnp.bfloat16
F32 = jnp.float32
LANES = 128
MIB = 2**20


def dot(a, b):
    return jnp.dot(a, b, preferred_element_type=F32)


def dot_nt(a, b):
    return lax.dot_general(a, b, (((1,), (1,)), ((), ())), preferred_element_type=F32)


def split_kernel(place_ref, green_ref, history_ref, green_out_ref, *refs):
    groups, sems = refs[:-1], refs[-1]
    columns = 1 << (len(groups) - 1)
    span = green_ref.shape[2]
    ratio = groups[0].shape[3] // span
    copies = [pltpu.make_async_copy(green_ref, green_out_ref, sems.at[columns, 0])]
    for d in range(columns):
        piece = groups[d.bit_length()].at[d - (1 << d.bit_length() >> 1)]
        for rho in range(ratio):
            at = pl.multiple_of((rho * columns + (place_ref[1] ^ d)) * span, span)
            copies.append(
                pltpu.make_async_copy(
                    history_ref.at[:, :, pl.ds(at, span)],
                    piece.at[:, :, pl.ds(rho * span, span)],
                    sems.at[d, rho],
                )
            )
    for copy in copies:
        copy.start()
    for copy in copies:
        copy.wait()


def split_history(place, green, history, col_devices):
    _, depth, width = history.shape
    span = green.shape[2]
    ratio = width // span // col_devices
    anywhere = pl.BlockSpec(memory_space=pl.ANY)
    sizes = [1, *bits(col_devices)]
    return pl.pallas_call(
        split_kernel,
        out_shape=[jax.ShapeDtypeStruct(green.shape, F32)]
        + [jax.ShapeDtypeStruct((n, 2, depth, ratio * span), BF16) for n in sizes],
        in_specs=[pl.BlockSpec(memory_space=pltpu.SMEM), anywhere, anywhere],
        out_specs=[anywhere] * (1 + len(sizes)),
        scratch_shapes=[pltpu.SemaphoreType.DMA((col_devices + 1, ratio))],
        compiler_params=pltpu.CompilerParams(vmem_limit_bytes=16 * MIB),
        name="split_history",
    )(
        place,
        pltpu.with_memory_space_constraint(green, pltpu.HBM),
        pltpu.with_memory_space_constraint(history, pltpu.HBM),
    )


def energy_kernel(orbitals, turn, green_ref, fit_ref, *refs):
    if turn:
        out_ref, turned_ref, tall_ref, spread, under, wide = refs
    else:
        turned_ref, tall_ref, out_ref, spread, under = refs
    aux, flat = fit_ref.shape
    times = green_ref.shape[2] // orbitals
    new = green_ref.shape[1] // orbitals
    pairs = new * times
    pitch = 2 * orbitals + 1
    per = LANES // orbitals
    flipped = [
        [green_ref[c, a * orbitals : (a + 1) * orbitals, :].T.astype(BF16) for c in range(2)]
        for a in range(new)
    ]
    lhs = jnp.concatenate([flipped[a][c] for a in range(new) for c in range(2)], axis=0)
    zero = jnp.zeros_like(lhs)
    both = [
        jnp.concatenate([lhs if q == h else zero for q in range(per)], axis=1) for h in range(per)
    ]
    for i in range(0, orbitals, 2 * per):
        if turn:
            for t in range(i // per, i // per + 2):
                at = slice(t * LANES, (t + 1) * LANES)
                wide[at, :] = fit_ref[:, at].astype(F32).T
                tall_ref[at, :] = wide[at, :].astype(BF16)
        w = jnp.concatenate(
            [fit_ref[:, (i + per * g) * orbitals : (i + per * (g + 1)) * orbitals] for g in range(2)],
            axis=0,
        )
        for h in range(per):
            res = dot_nt(both[h], w)
            for g in range(2):
                for a in range(new):
                    for c in range(2):
                        for k in range(times):
                            r = ((a * 2 + c) * times + k) * orbitals
                            spread[
                                a * times + k,
                                pl.ds(c * orbitals + i + per * g + h, orbitals, stride=pitch),
                                :,
                            ] = res[r : r + orbitals, g * aux : (g + 1) * aux]
    around = [jnp.concatenate(flipped[a], axis=1) for a in range(new)]
    rows = 2 * orbitals
    group = 2
    for m in range(0, orbitals, 2):
        if turn and m % per == 0:
            x = [wide[pl.ds(m + h, orbitals, stride=orbitals), :] for h in range(per)]
            at = slice(m * orbitals, (m + per) * orbitals)
            turned_ref[:, at] = jnp.concatenate(x, axis=0).T.astype(BF16)
        for n in range(pairs):
            a, k = divmod(n, times)
            x = [spread[n, pl.ds((m + h) * pitch, rows), :].astype(BF16) for h in range(2)]
            r = dot(around[a][k * orbitals : (k + 1) * orbitals], jnp.concatenate(x, axis=1))
            for h in range(2):
                under[(m + h) * orbitals : (m + h + 1) * orbitals, n * aux : (n + 1) * aux] = r[
                    :, h * aux : (h + 1) * aux
                ].astype(BF16)
    bubble = dot(turned_ref[...], under[...]) * (1.0 / orbitals)
    screened = under
    screened[...] = dot(tall_ref[...], bubble.astype(BF16)).astype(BF16)
    scale = (aux * orbitals) ** -0.5
    for n in range(pairs):
        acc = jnp.zeros((orbitals, rows), F32)
        for l in range(0, orbitals, group):
            a = [
                screened[(l + h) * orbitals : (l + h + 1) * orbitals, n * aux : (n + 1) * aux]
                for h in range(group)
            ]
            b = [spread[n, pl.ds((l + h) * pitch, rows), :].astype(BF16) for h in range(group)]
            acc = acc + dot_nt(jnp.concatenate(a, axis=1), jnp.concatenate(b, axis=1))
        block = (acc * scale).T.astype(BF16)
        a, k = divmod(n, times)
        for c in range(2):
            out_ref[
                c, a * orbitals : (a + 1) * orbitals, k * orbitals : (k + 1) * orbitals
            ] = block[c * orbitals : (c + 1) * orbitals]


def energy(green, fit, turned, orbitals):
    aux, flat = fit.shape
    _, rows, span = green.shape
    pairs = rows // orbitals * (span // orbitals)
    turn = turned is None
    out_shape = jax.ShapeDtypeStruct((2, rows, span), BF16)
    forms = [jax.ShapeDtypeStruct((aux, flat), BF16), jax.ShapeDtypeStruct((flat, aux), BF16)]
    scratch = [
        pltpu.VMEM((pairs, orbitals * (2 * orbitals + 1), aux), F32),
        pltpu.VMEM((flat, pairs * aux), BF16),
    ]
    return pl.pallas_call(
        functools.partial(energy_kernel, orbitals, turn),
        out_shape=[out_shape, *forms] if turn else out_shape,
        scratch_shapes=scratch + [pltpu.VMEM((flat, aux), F32)] * turn,
        compiler_params=pltpu.CompilerParams(vmem_limit_bytes=28 * MIB),
        name="self_energy",
    )(green, fit, *(() if turn else turned))


def collide_kernel(offsets, row_devices, place_ref, near_ref, far_ref, *refs):
    pieces, keep_ref, sends, sums = refs[: -row_devices - 1], refs[-row_devices - 1], refs[-row_devices:-1], refs[-1]
    row, col = place_ref[0], place_ref[1]
    _, _, rows, span = near_ref.shape
    half = near_ref.shape[0]
    ratio = row_devices // len(pieces)
    blocks = []
    for b in range(2 * half):
        ref, at = (near_ref, b) if b < half else (far_ref, b - half)
        blocks.append(jnp.concatenate([ref[at, c] for c in range(2)], axis=0))
    stacked = jnp.concatenate(blocks, axis=1)
    for s, piece in enumerate(pieces):
        depth = []
        for offset in offsets:
            at = pl.ds(pl.multiple_of((col ^ offset) * span, span), span)
            depth.append(jnp.concatenate([piece[0, c, at, :] for c in range(2)], axis=1))
        acc = dot(stacked, jnp.concatenate(depth, axis=0))
        width = ratio * span
        real = acc[:rows, :width] - acc[rows:, width:]
        imag = acc[:rows, width:] + acc[rows:, :width]
        for rho in range(ratio):
            t = ((col ^ s) * ratio + rho) ^ row
            sums[t, 0] = real[:, rho * span : (rho + 1) * span]
            sums[t, 1] = imag[:, rho * span : (rho + 1) * span]
    keep_ref[...] = sums[0]
    for t in range(1, row_devices):
        sends[t - 1][...] = sums[t].astype(BF16)


def collide(place, near, far, pieces, offsets, row_devices):
    _, _, rows, span = near.shape
    shape = (2, rows, span)
    return pl.pallas_call(
        functools.partial(collide_kernel, offsets, row_devices),
        grid=(1,),
        out_shape=[jax.ShapeDtypeStruct(shape, F32)]
        + [jax.ShapeDtypeStruct(shape, BF16)] * (row_devices - 1),
        in_specs=[pl.BlockSpec(memory_space=pltpu.SMEM)]
        + [pl.BlockSpec(memory_space=pltpu.VMEM)] * 2
        + [pl.BlockSpec((1, *piece.shape[1:]), lambda _: (0, 0, 0, 0)) for piece in pieces],
        scratch_shapes=[pltpu.VMEM((row_devices, 2, rows, span), F32)],
        compiler_params=pltpu.CompilerParams(vmem_limit_bytes=32 * MIB),
        name="collide",
    )(place, near, far, *pieces)


def swap(x, axis, step):
    size = lax.axis_size(axis)
    return lax.ppermute(x, axis, [(d, d ^ step) for d in range(size)])


def bits(size):
    return [1 << b for b in range(size.bit_length() - 1)]


def local(green_start, fit, history):
    orbitals = math.isqrt(fit.shape[1])
    row_devices = lax.axis_size("row")
    col_devices = lax.axis_size("col")
    place = jnp.stack([lax.axis_index("row"), lax.axis_index("col")]).astype(jnp.int32)

    green_start, kept, *groups = split_history(place, green_start, history, col_devices)
    held = {0: kept}

    def pass_on(step):
        for offset, array in list(held.items()):
            if array.shape[0] > step:
                held[offset ^ step] = swap(array[step : 2 * step], "col", step)
        held[step] = swap(groups.pop(), "col", step)

    steps = bits(col_devices)[::-1]
    pass_on(steps[0])
    green, turned = green_start, None
    for _ in range(ITERS):
        if turned is None:
            sigma, *turned = energy(green, fit, None, orbitals)
        else:
            sigma = energy(green, fit, turned, orbitals)
        near, offsets = sigma[None], [0]
        far = None
        for step in steps:
            if far is not None:
                near = jnp.concatenate([near, far], axis=0)
            far = swap(near, "col", step)
            if held:
                far, held = lax.optimization_barrier((far, held))
                for later in steps[1:]:
                    pass_on(later)
                pieces, held = [held[offset] for offset in range(col_devices)], None
            offsets = offsets + [o ^ step for o in offsets]
        keep, *sends = collide(place, near, far, pieces, offsets, row_devices)
        green = green_start + keep
        for step in sorted(range(1, row_devices), key=lambda t: -(t ^ 1)):
            green = green + swap(sends[step - 1], "row", step).astype(F32)
    return green


def solution(mesh):
    in_specs = (P("groups", None, ("row", "col")), P("groups", None), P("groups", "row", "col"))
    out_specs = P("groups", None, ("row", "col"))
    return jax.shard_map(local, mesh=mesh, in_specs=in_specs, out_specs=out_specs, check_vma=False)
```

```python
import functools
import math

import jax
import jax.numpy as jnp
from jax import lax
from jax.experimental import pallas as pl
from jax.experimental.pallas import tpu as pltpu
from jax.sharding import PartitionSpec as P

ITERS = 2
BF16 = jnp.bfloat16
F32 = jnp.float32
LANES = 128
MIB = 2**20


def dot(a, b):
    return jnp.dot(a, b, preferred_element_type=F32)


def dot_nt(a, b):
    return lax.dot_general(a, b, (((1,), (1,)), ((), ())), preferred_element_type=F32)


def split_kernel(place_ref, green_ref, history_ref, green_out_ref, *refs):
    groups, sems = refs[:-1], refs[-1]
    columns = 1 << (len(groups) - 1)
    span = green_ref.shape[2]
    ratio = groups[0].shape[3] // span
    copies = [pltpu.make_async_copy(green_ref, green_out_ref, sems.at[columns, 0])]
    for d in range(columns):
        piece = groups[d.bit_length()].at[d - (1 << d.bit_length() >> 1)]
        for rho in range(ratio):
            at = pl.multiple_of((rho * columns + (place_ref[1] ^ d)) * span, span)
            copies.append(
                pltpu.make_async_copy(
                    history_ref.at[:, :, pl.ds(at, span)],
                    piece.at[:, :, pl.ds(rho * span, span)],
                    sems.at[d, rho],
                )
            )
    for copy in copies:
        copy.start()
    for copy in copies:
        copy.wait()


def split_history(place, green, history, col_devices):
    _, depth, width = history.shape
    span = green.shape[2]
    ratio = width // span // col_devices
    anywhere = pl.BlockSpec(memory_space=pl.ANY)
    sizes = [1, *bits(col_devices)]
    return pl.pallas_call(
        split_kernel,
        out_shape=[jax.ShapeDtypeStruct(green.shape, F32)]
        + [jax.ShapeDtypeStruct((n, 2, depth, ratio * span), BF16) for n in sizes],
        in_specs=[pl.BlockSpec(memory_space=pltpu.SMEM), anywhere, anywhere],
        out_specs=[anywhere] * (1 + len(sizes)),
        scratch_shapes=[pltpu.SemaphoreType.DMA((col_devices + 1, ratio))],
        compiler_params=pltpu.CompilerParams(vmem_limit_bytes=16 * MIB),
        name="split_history",
    )(
        place,
        pltpu.with_memory_space_constraint(green, pltpu.HBM),
        pltpu.with_memory_space_constraint(history, pltpu.HBM),
    )


def energy_kernel(orbitals, turn, green_ref, fit_ref, *refs):
    if turn:
        out_ref, turned_ref, tall_ref, spread, under, wide = refs
    else:
        turned_ref, tall_ref, out_ref, spread, under = refs
    aux, flat = fit_ref.shape
    times = green_ref.shape[2] // orbitals
    new = green_ref.shape[1] // orbitals
    pairs = new * times
    pitch = 2 * orbitals + 1
    per = LANES // orbitals
    flipped = [
        [green_ref[c, a * orbitals : (a + 1) * orbitals, :].T.astype(BF16) for c in range(2)]
        for a in range(new)
    ]
    lhs = jnp.concatenate([flipped[a][c] for a in range(new) for c in range(2)], axis=0)
    zero = jnp.zeros_like(lhs)
    both = [
        jnp.concatenate([lhs if q == h else zero for q in range(per)], axis=1) for h in range(per)
    ]
    for i in range(0, orbitals, 2 * per):
        if turn:
            for t in range(i // per, i // per + 2):
                at = slice(t * LANES, (t + 1) * LANES)
                y = fit_ref[:, at].astype(F32).T
                tall_ref[at, :] = y.astype(BF16)
                for h in range(per):
                    r = (t * per + h) * (orbitals + 1)
                    wide[r : r + orbitals, :] = y[h * orbitals : (h + 1) * orbitals]
        w = jnp.concatenate(
            [fit_ref[:, (i + per * g) * orbitals : (i + per * (g + 1)) * orbitals] for g in range(2)],
            axis=0,
        )
        for h in range(per):
            res = dot_nt(both[h], w)
            for g in range(2):
                for a in range(new):
                    for c in range(2):
                        for k in range(times):
                            r = ((a * 2 + c) * times + k) * orbitals
                            spread[
                                a * times + k,
                                pl.ds(c * orbitals + i + per * g + h, orbitals, stride=pitch),
                                :,
                            ] = res[r : r + orbitals, g * aux : (g + 1) * aux]
    around = [jnp.concatenate(flipped[a], axis=1) for a in range(new)]
    rows = 2 * orbitals
    group = 2
    for m in range(0, orbitals, 2):
        if turn and m % per == 0:
            x = [wide[pl.ds(m + h, orbitals, stride=orbitals + 1), :] for h in range(per)]
            at = slice(m * orbitals, (m + per) * orbitals)
            turned_ref[:, at] = jnp.concatenate(x, axis=0).T.astype(BF16)
        for n in range(pairs):
            a, k = divmod(n, times)
            x = [spread[n, pl.ds((m + h) * pitch, rows), :].astype(BF16) for h in range(2)]
            r = dot(around[a][k * orbitals : (k + 1) * orbitals], jnp.concatenate(x, axis=1))
            for h in range(2):
                under[(m + h) * orbitals : (m + h + 1) * orbitals, n * aux : (n + 1) * aux] = r[
                    :, h * aux : (h + 1) * aux
                ].astype(BF16)
    bubble = dot(turned_ref[...], under[...]) * (1.0 / orbitals)
    screened = under
    screened[...] = dot(tall_ref[...], bubble.astype(BF16)).astype(BF16)
    scale = (aux * orbitals) ** -0.5
    for n in range(pairs):
        acc = jnp.zeros((orbitals, rows), F32)
        for l in range(0, orbitals, group):
            a = [
                screened[(l + h) * orbitals : (l + h + 1) * orbitals, n * aux : (n + 1) * aux]
                for h in range(group)
            ]
            b = [spread[n, pl.ds((l + h) * pitch, rows), :].astype(BF16) for h in range(group)]
            acc = acc + dot_nt(jnp.concatenate(a, axis=1), jnp.concatenate(b, axis=1))
        block = (acc * scale).T.astype(BF16)
        a, k = divmod(n, times)
        for c in range(2):
            out_ref[
                c, a * orbitals : (a + 1) * orbitals, k * orbitals : (k + 1) * orbitals
            ] = block[c * orbitals : (c + 1) * orbitals]


def energy(green, fit, turned, orbitals):
    aux, flat = fit.shape
    _, rows, span = green.shape
    pairs = rows // orbitals * (span // orbitals)
    turn = turned is None
    out_shape = jax.ShapeDtypeStruct((2, rows, span), BF16)
    forms = [jax.ShapeDtypeStruct((aux, flat), BF16), jax.ShapeDtypeStruct((flat, aux), BF16)]
    scratch = [
        pltpu.VMEM((pairs, orbitals * (2 * orbitals + 1), aux), F32),
        pltpu.VMEM((flat, pairs * aux), BF16),
    ]
    return pl.pallas_call(
        functools.partial(energy_kernel, orbitals, turn),
        out_shape=[out_shape, *forms] if turn else out_shape,
        scratch_shapes=scratch + [pltpu.VMEM((orbitals * (orbitals + 1), aux), F32)] * turn,
        compiler_params=pltpu.CompilerParams(vmem_limit_bytes=34 * MIB),
        name="self_energy",
    )(green, fit, *(() if turn else turned))


def collide_kernel(offsets, row_devices, place_ref, near_ref, far_ref, *refs):
    pieces, keep_ref, sends, sums = refs[: -row_devices - 1], refs[-row_devices - 1], refs[-row_devices:-1], refs[-1]
    row, col = place_ref[0], place_ref[1]
    _, _, rows, span = near_ref.shape
    half = near_ref.shape[0]
    ratio = row_devices // len(pieces)
    blocks = []
    for b in range(2 * half):
        ref, at = (near_ref, b) if b < half else (far_ref, b - half)
        blocks.append(jnp.concatenate([ref[at, c] for c in range(2)], axis=0))
    stacked = jnp.concatenate(blocks, axis=1)
    for s, piece in enumerate(pieces):
        depth = []
        for offset in offsets:
            at = pl.ds(pl.multiple_of((col ^ offset) * span, span), span)
            depth.append(jnp.concatenate([piece[0, c, at, :] for c in range(2)], axis=1))
        acc = dot(stacked, jnp.concatenate(depth, axis=0))
        width = ratio * span
        real = acc[:rows, :width] - acc[rows:, width:]
        imag = acc[:rows, width:] + acc[rows:, :width]
        for rho in range(ratio):
            t = ((col ^ s) * ratio + rho) ^ row
            sums[t, 0] = real[:, rho * span : (rho + 1) * span]
            sums[t, 1] = imag[:, rho * span : (rho + 1) * span]
    keep_ref[...] = sums[0]
    for t in range(1, row_devices):
        sends[t - 1][...] = sums[t].astype(BF16)


def collide(place, near, far, pieces, offsets, row_devices):
    _, _, rows, span = near.shape
    shape = (2, rows, span)
    return pl.pallas_call(
        functools.partial(collide_kernel, offsets, row_devices),
        grid=(1,),
        out_shape=[jax.ShapeDtypeStruct(shape, F32)]
        + [jax.ShapeDtypeStruct(shape, BF16)] * (row_devices - 1),
        in_specs=[pl.BlockSpec(memory_space=pltpu.SMEM)]
        + [pl.BlockSpec(memory_space=pltpu.VMEM)] * 2
        + [pl.BlockSpec((1, *piece.shape[1:]), lambda _: (0, 0, 0, 0)) for piece in pieces],
        scratch_shapes=[pltpu.VMEM((row_devices, 2, rows, span), F32)],
        compiler_params=pltpu.CompilerParams(vmem_limit_bytes=32 * MIB),
        name="collide",
    )(place, near, far, *pieces)


def swap(x, axis, step):
    size = lax.axis_size(axis)
    return lax.ppermute(x, axis, [(d, d ^ step) for d in range(size)])


def bits(size):
    return [1 << b for b in range(size.bit_length() - 1)]


def local(green_start, fit, history):
    orbitals = math.isqrt(fit.shape[1])
    row_devices = lax.axis_size("row")
    col_devices = lax.axis_size("col")
    place = jnp.stack([lax.axis_index("row"), lax.axis_index("col")]).astype(jnp.int32)

    green_start, kept, *groups = split_history(place, green_start, history, col_devices)
    held = {0: kept}

    def pass_on(step):
        for offset, array in list(held.items()):
            if array.shape[0] > step:
                held[offset ^ step] = swap(array[step : 2 * step], "col", step)
        held[step] = swap(groups.pop(), "col", step)

    steps = bits(col_devices)[::-1]
    pass_on(steps[0])
    green, turned = green_start, None
    for _ in range(ITERS):
        if turned is None:
            sigma, *turned = energy(green, fit, None, orbitals)
        else:
            sigma = energy(green, fit, turned, orbitals)
        near, offsets = sigma[None], [0]
        far = None
        for step in steps:
            if far is not None:
                near = jnp.concatenate([near, far], axis=0)
            far = swap(near, "col", step)
            if held:
                far, held = lax.optimization_barrier((far, held))
                for later in steps[1:]:
                    pass_on(later)
                pieces, held = [held[offset] for offset in range(col_devices)], None
            offsets = offsets + [o ^ step for o in offsets]
        keep, *sends = collide(place, near, far, pieces, offsets, row_devices)
        green = green_start + keep
        for step in sorted(range(1, row_devices), key=lambda t: -(t ^ 1)):
            green = green + swap(sends[step - 1], "row", step).astype(F32)
    return green


def solution(mesh):
    in_specs = (P("groups", None, ("row", "col")), P("groups", None), P("groups", "row", "col"))
    out_specs = P("groups", None, ("row", "col"))
    return jax.shard_map(local, mesh=mesh, in_specs=in_specs, out_specs=out_specs, check_vma=False)
```

```python
import functools
import math

import jax
import jax.numpy as jnp
from jax import lax
from jax.experimental import pallas as pl
from jax.experimental.pallas import tpu as pltpu
from jax.sharding import PartitionSpec as P

ITERS = 2
BF16 = jnp.bfloat16
F32 = jnp.float32
LANES = 128
MIB = 2**20


def dot(a, b):
    return jnp.dot(a, b, preferred_element_type=F32)


def dot_nt(a, b):
    return lax.dot_general(a, b, (((1,), (1,)), ((), ())), preferred_element_type=F32)


def split_kernel(place_ref, green_ref, history_ref, green_out_ref, *refs):
    groups, sems = refs[:-1], refs[-1]
    columns = 1 << (len(groups) - 1)
    span = green_ref.shape[2]
    ratio = groups[0].shape[3] // span
    copies = [pltpu.make_async_copy(green_ref, green_out_ref, sems.at[columns, 0])]
    for d in range(columns):
        piece = groups[d.bit_length()].at[d - (1 << d.bit_length() >> 1)]
        for rho in range(ratio):
            at = pl.multiple_of((rho * columns + (place_ref[1] ^ d)) * span, span)
            copies.append(
                pltpu.make_async_copy(
                    history_ref.at[:, :, pl.ds(at, span)],
                    piece.at[:, :, pl.ds(rho * span, span)],
                    sems.at[d, rho],
                )
            )
    for copy in copies:
        copy.start()
    for copy in copies:
        copy.wait()


def split_history(place, green, history, col_devices):
    _, depth, width = history.shape
    span = green.shape[2]
    ratio = width // span // col_devices
    anywhere = pl.BlockSpec(memory_space=pl.ANY)
    sizes = [1, *bits(col_devices)]
    return pl.pallas_call(
        split_kernel,
        out_shape=[jax.ShapeDtypeStruct(green.shape, F32)]
        + [jax.ShapeDtypeStruct((n, 2, depth, ratio * span), BF16) for n in sizes],
        in_specs=[pl.BlockSpec(memory_space=pltpu.SMEM), anywhere, anywhere],
        out_specs=[anywhere] * (1 + len(sizes)),
        scratch_shapes=[pltpu.SemaphoreType.DMA((col_devices + 1, ratio))],
        compiler_params=pltpu.CompilerParams(vmem_limit_bytes=16 * MIB),
        name="split_history",
    )(
        place,
        pltpu.with_memory_space_constraint(green, pltpu.HBM),
        pltpu.with_memory_space_constraint(history, pltpu.HBM),
    )


def energy_kernel(orbitals, turn, green_ref, fit_ref, *refs):
    if turn:
        out_ref, turned_ref, tall_ref, spread, under, wide = refs
    else:
        turned_ref, tall_ref, out_ref, spread, under = refs
    aux, flat = fit_ref.shape
    times = green_ref.shape[2] // orbitals
    new = green_ref.shape[1] // orbitals
    pairs = new * times
    pitch = 2 * orbitals + 1
    per = LANES // orbitals
    flipped = [
        [green_ref[c, a * orbitals : (a + 1) * orbitals, :].T.astype(BF16) for c in range(2)]
        for a in range(new)
    ]
    lhs = jnp.concatenate([flipped[a][c] for a in range(new) for c in range(2)], axis=0)
    zero = jnp.zeros_like(lhs)
    both = [
        jnp.concatenate([lhs if q == h else zero for q in range(per)], axis=1) for h in range(per)
    ]
    for i in range(0, orbitals, 2 * per):
        if turn:
            for t in range(i // per, i // per + 2):
                at = slice(t * LANES, (t + 1) * LANES)
                y = fit_ref[:, at].astype(F32).T
                tall_ref[at, :] = y.astype(BF16)
                for h in range(per):
                    r = (t * per + h) * (orbitals + 1)
                    wide[r : r + orbitals, :] = y[h * orbitals : (h + 1) * orbitals]
        w = jnp.concatenate(
            [fit_ref[:, (i + per * g) * orbitals : (i + per * (g + 1)) * orbitals] for g in range(2)],
            axis=0,
        )
        for h in range(per):
            res = dot_nt(both[h], w)
            for g in range(2):
                for a in range(new):
                    for c in range(2):
                        for k in range(times):
                            r = ((a * 2 + c) * times + k) * orbitals
                            spread[
                                a * times + k,
                                pl.ds(c * orbitals + i + per * g + h, orbitals, stride=pitch),
                                :,
                            ] = res[r : r + orbitals, g * aux : (g + 1) * aux]
    around = [jnp.concatenate(flipped[a], axis=1) for a in range(new)]
    rows = 2 * orbitals
    group = 2
    for m in range(0, orbitals, 2):
        if turn and m % per == 0:
            x = [wide[pl.ds(m + h, orbitals, stride=orbitals + 1), :] for h in range(per)]
            at = slice(m * orbitals, (m + per) * orbitals)
            turned_ref[:, at] = jnp.concatenate(x, axis=0).T.astype(BF16)
        for n in range(pairs):
            a, k = divmod(n, times)
            x = [spread[n, pl.ds((m + h) * pitch, rows), :].astype(BF16) for h in range(2)]
            r = dot(around[a][k * orbitals : (k + 1) * orbitals], jnp.concatenate(x, axis=1))
            for h in range(2):
                under[(m + h) * orbitals : (m + h + 1) * orbitals, n * aux : (n + 1) * aux] = r[
                    :, h * aux : (h + 1) * aux
                ].astype(BF16)
    bubble = dot(turned_ref[...], under[...]) * (1.0 / orbitals)
    screened = under
    screened[...] = dot(tall_ref[...], bubble.astype(BF16)).astype(BF16)
    scale = (aux * orbitals) ** -0.5
    for n in range(pairs):
        acc = jnp.zeros((orbitals, rows), F32)
        for l in range(0, orbitals, group):
            a = [
                screened[(l + h) * orbitals : (l + h + 1) * orbitals, n * aux : (n + 1) * aux]
                for h in range(group)
            ]
            b = [spread[n, pl.ds((l + h) * pitch, rows), :].astype(BF16) for h in range(group)]
            acc = acc + dot_nt(jnp.concatenate(a, axis=1), jnp.concatenate(b, axis=1))
        block = (acc * scale).T.astype(BF16)
        a, k = divmod(n, times)
        for c in range(2):
            out_ref[
                c, a * orbitals : (a + 1) * orbitals, k * orbitals : (k + 1) * orbitals
            ] = block[c * orbitals : (c + 1) * orbitals]


def energy(green, fit, turned, orbitals):
    aux, flat = fit.shape
    _, rows, span = green.shape
    pairs = rows // orbitals * (span // orbitals)
    turn = turned is None
    out_shape = jax.ShapeDtypeStruct((2, rows, span), BF16)
    forms = [jax.ShapeDtypeStruct((aux, flat), BF16), jax.ShapeDtypeStruct((flat, aux), BF16)]
    scratch = [
        pltpu.VMEM((pairs, (orbitals + 1) * (2 * orbitals + 1), aux), F32),
        pltpu.VMEM((flat, pairs * aux), BF16),
    ]
    return pl.pallas_call(
        functools.partial(energy_kernel, orbitals, turn),
        out_shape=[out_shape, *forms] if turn else out_shape,
        scratch_shapes=scratch + [pltpu.VMEM((orbitals * (orbitals + 2), aux), F32)] * turn,
        compiler_params=pltpu.CompilerParams(vmem_limit_bytes=34 * MIB),
        name="self_energy",
    )(green, fit, *(() if turn else turned))


def collide_kernel(offsets, row_devices, place_ref, near_ref, far_ref, *refs):
    pieces, keep_ref, sends, sums = refs[: -row_devices - 1], refs[-row_devices - 1], refs[-row_devices:-1], refs[-1]
    row, col = place_ref[0], place_ref[1]
    _, _, rows, span = near_ref.shape
    half = near_ref.shape[0]
    ratio = row_devices // len(pieces)
    blocks = []
    for b in range(2 * half):
        ref, at = (near_ref, b) if b < half else (far_ref, b - half)
        blocks.append(jnp.concatenate([ref[at, c] for c in range(2)], axis=0))
    stacked = jnp.concatenate(blocks, axis=1)
    for s, piece in enumerate(pieces):
        depth = []
        for offset in offsets:
            at = pl.ds(pl.multiple_of((col ^ offset) * span, span), span)
            depth.append(jnp.concatenate([piece[0, c, at, :] for c in range(2)], axis=1))
        acc = dot(stacked, jnp.concatenate(depth, axis=0))
        width = ratio * span
        real = acc[:rows, :width] - acc[rows:, width:]
        imag = acc[:rows, width:] + acc[rows:, :width]
        for rho in range(ratio):
            t = ((col ^ s) * ratio + rho) ^ row
            sums[t, 0] = real[:, rho * span : (rho + 1) * span]
            sums[t, 1] = imag[:, rho * span : (rho + 1) * span]
    keep_ref[...] = sums[0]
    for t in range(1, row_devices):
        sends[t - 1][...] = sums[t].astype(BF16)


def collide(place, near, far, pieces, offsets, row_devices):
    _, _, rows, span = near.shape
    shape = (2, rows, span)
    return pl.pallas_call(
        functools.partial(collide_kernel, offsets, row_devices),
        grid=(1,),
        out_shape=[jax.ShapeDtypeStruct(shape, F32)]
        + [jax.ShapeDtypeStruct(shape, BF16)] * (row_devices - 1),
        in_specs=[pl.BlockSpec(memory_space=pltpu.SMEM)]
        + [pl.BlockSpec(memory_space=pltpu.VMEM)] * 2
        + [pl.BlockSpec((1, *piece.shape[1:]), lambda _: (0, 0, 0, 0)) for piece in pieces],
        scratch_shapes=[pltpu.VMEM((row_devices, 2, rows, span), F32)],
        compiler_params=pltpu.CompilerParams(vmem_limit_bytes=32 * MIB),
        name="collide",
    )(place, near, far, *pieces)


def swap(x, axis, step):
    size = lax.axis_size(axis)
    return lax.ppermute(x, axis, [(d, d ^ step) for d in range(size)])


def bits(size):
    return [1 << b for b in range(size.bit_length() - 1)]


def local(green_start, fit, history):
    orbitals = math.isqrt(fit.shape[1])
    row_devices = lax.axis_size("row")
    col_devices = lax.axis_size("col")
    place = jnp.stack([lax.axis_index("row"), lax.axis_index("col")]).astype(jnp.int32)

    green_start, kept, *groups = split_history(place, green_start, history, col_devices)
    held = {0: kept}

    def pass_on(step):
        for offset, array in list(held.items()):
            if array.shape[0] > step:
                held[offset ^ step] = swap(array[step : 2 * step], "col", step)
        held[step] = swap(groups.pop(), "col", step)

    steps = bits(col_devices)[::-1]
    pass_on(steps[0])
    green, turned = green_start, None
    for _ in range(ITERS):
        if turned is None:
            sigma, *turned = energy(green, fit, None, orbitals)
        else:
            sigma = energy(green, fit, turned, orbitals)
        near, offsets = sigma[None], [0]
        far = None
        for step in steps:
            if far is not None:
                near = jnp.concatenate([near, far], axis=0)
            far = swap(near, "col", step)
            if held:
                far, held = lax.optimization_barrier((far, held))
                for later in steps[1:]:
                    pass_on(later)
                pieces, held = [held[offset] for offset in range(col_devices)], None
            offsets = offsets + [o ^ step for o in offsets]
        keep, *sends = collide(place, near, far, pieces, offsets, row_devices)
        green = green_start + keep
        for step in sorted(range(1, row_devices), key=lambda t: -(t ^ 1)):
            green = green + swap(sends[step - 1], "row", step).astype(F32)
    return green


def solution(mesh):
    in_specs = (P("groups", None, ("row", "col")), P("groups", None), P("groups", "row", "col"))
    out_specs = P("groups", None, ("row", "col"))
    return jax.shard_map(local, mesh=mesh, in_specs=in_specs, out_specs=out_specs, check_vma=False)
```
